128 devices in a mesh: rep: 4 (over y), fsdp: 32 (over x, z, core).
Axes of the slice: x: 4, y: 4, z: 4, core: 2. Of those that a mesh axis runs over, the one named last changes fastest.
Arguments:
- grads: bfloat16 [4, 12, 1024, 5120], P('rep', None, 'fsdp'), may hold values from -0.75 to 0.75
- stat_left: float32 [128, 1024, 1024], P(('rep', 'fsdp')), may hold values from -4 to 80
- stat_right: float32 [128, 1024, 1024], P(('rep', 'fsdp')), may hold values from -4 to 80
- root_left: bfloat16 [128, 1024, 1024], P(('rep', 'fsdp')), may hold values from -0.125 to 1.203125
- root_right: bfloat16 [128, 1024, 1024], P(('rep', 'fsdp')), may hold values from -0.125 to 1.203125
- owner_block: int32 [128], replicated, may hold values from -1 to 59, as said below
Outputs:
- stat_left_new: float32 [128, 1024, 1024], P(('rep', 'fsdp'))
- stat_right_new: float32 [128, 1024, 1024], P(('rep', 'fsdp'))
- update: bfloat16 [12, 1024, 5120], P(None, ('rep', 'fsdp'))
The draws below stay inside these ranges and needn't reach their ends.
Inputs may be any that keep to these rules, and one draw needn't show every extreme that they name: `owner_block`: entry d is the block whose preconditioner owner d holds, or -1 where it holds none; each block 0 to 59 appears exactly once.
All inputs are finite; a program needn't handle non-finite values.
Results may differ from the reference program's by a relative error of at most 0.017.
Values may be sent and summed in bfloat16 or wider, within the bound.
No kernel may reach another device: no remote copies, remote signals or barrier semaphores. Data moves between devices by JAX's collectives and lax.ppermute only.
A program may use at most 128 MiB of HBM per device.

```python
import math
import jax
import jax.numpy as jnp
from jax import lax

D = 5120
BS = 1024
ROW_GROUPS = 12
BLOCKS = 60
N_REP = 4
DEVICES = 128


def assemble(noise, diagonal, off_norm):
    size = noise.shape[-1]
    mixed = (noise + jnp.swapaxes(noise, 1, 2)) * (off_norm / math.sqrt(2.0 * size))
    row_index = lax.broadcasted_iota(jnp.int32, noise.shape, 1)
    col_index = lax.broadcasted_iota(jnp.int32, noise.shape, 2)
    return jnp.where(row_index == col_index, diagonal[:, :, None], mixed)


def draw_stat_left(key, part):
    key = jax.random.fold_in(key, 11)
    noise_key, diag_key = jax.random.split(key)
    shape = (DEVICES, BS, BS)
    noise = jnp.clip(jax.random.normal(noise_key, shape, jnp.float32), -4.0, 4.0)
    diagonal = jax.random.uniform(diag_key, (DEVICES, BS), jnp.float32, 20.0, 80.0)
    return assemble(noise, diagonal, 8.0)


def draw_stat_right(key, part):
    key = jax.random.fold_in(key, 23)
    noise_key, diag_key = jax.random.split(key)
    shape = (DEVICES, BS, BS)
    noise = jnp.clip(jax.random.normal(noise_key, shape, jnp.float32), -4.0, 4.0)
    diagonal = jax.random.uniform(diag_key, (DEVICES, BS), jnp.float32, 20.0, 80.0)
    return assemble(noise, diagonal, 8.0)


def draw_root_left(key, part):
    key = jax.random.fold_in(key, 37)
    noise_key, diag_key = jax.random.split(key)
    shape = (DEVICES, BS, BS)
    noise = jnp.clip(jax.random.normal(noise_key, shape, jnp.float32), -4.0, 4.0)
    diagonal = jax.random.uniform(diag_key, (DEVICES, BS), jnp.float32, 0.6, 1.2)
    return assemble(noise, diagonal, 0.25).astype(jnp.bfloat16)


def draw_root_right(key, part):
    key = jax.random.fold_in(key, 41)
    noise_key, diag_key = jax.random.split(key)
    shape = (DEVICES, BS, BS)
    noise = jnp.clip(jax.random.normal(noise_key, shape, jnp.float32), -4.0, 4.0)
    diagonal = jax.random.uniform(diag_key, (DEVICES, BS), jnp.float32, 0.6, 1.2)
    return assemble(noise, diagonal, 0.25).astype(jnp.bfloat16)


def draw_owner_block(key, part):
    key = jax.random.fold_in(key, 53)
    shuffled = jax.random.permutation(key, DEVICES).astype(jnp.int32)
    return jnp.where(shuffled < BLOCKS, shuffled, -1).astype(jnp.int32)


def levels(rng, shape, pieces, least, high):
    factor_of = 1.0
    for position, shards_of in pieces:
        steps = jax.random.uniform(jax.random.fold_in(jax.random.fold_in(rng, 6), position), (shards_of,), jnp.float32, least / len(pieces), high / len(pieces))
        factor_of = factor_of * jnp.repeat(jnp.exp(steps), shape[position] // shards_of).reshape((-1,) + (1,) * (len(shape) - 1 - position))
    return factor_of


def scatter_about(stream_key, extent, spread, bound, cuts=(), kind=jnp.bfloat16):
    factor_of = levels(stream_key, extent, cuts, -0.22, 0.18) if cuts else 1.0
    entries = jax.random.normal(stream_key, extent, jnp.float32) * spread * factor_of
    return jnp.minimum(jnp.maximum(entries, -bound), bound).astype(kind)


def setup_inputs(seed: int = 0) -> dict:
    seeds = jax.random.split(jax.random.key(seed), 7)
    grads = scatter_about(seeds[0], (N_REP, ROW_GROUPS, BS, D), 0.125, 0.75, ((0, 4), (2, 32)))
    stat_left = draw_stat_left(jax.random.fold_in(seeds[6], 71), 0)
    stat_right = draw_stat_right(jax.random.fold_in(seeds[6], 71), 0)
    root_left = draw_root_left(jax.random.fold_in(seeds[6], 71), 0)
    root_right = draw_root_right(jax.random.fold_in(seeds[6], 71), 0)
    owner_block = draw_owner_block(jax.random.fold_in(seeds[6], 71), 0)
    return {"grads": grads, "stat_left": stat_left, "stat_right": stat_right, "root_left": root_left, "root_right": root_right, "owner_block": owner_block}


DECAY = 0.95
EPSILON = 1e-06

def reference(grads, stat_left, stat_right, root_left, root_right, owner_block):
    columns = D // BS
    summed = lax.optimization_barrier(jnp.sum(grads.astype(jnp.float32), axis=0)).astype(jnp.bfloat16)
    blocks = summed.reshape(ROW_GROUPS, BS, columns, BS).transpose(0, 2, 1, 3).reshape(BLOCKS, BS, BS)

    def per_owner(operand_set):
        block_id, left_old, right_old, left_root, right_root = operand_set

        def occupied_case(unused):
            grad_block = blocks[jnp.maximum(block_id, 0)]
            gram_left = jnp.dot(grad_block, grad_block.T, preferred_element_type=jnp.float32)
            gram_right = jnp.dot(grad_block.T, grad_block, preferred_element_type=jnp.float32)
            middle = jnp.dot(left_root, grad_block, preferred_element_type=jnp.float32).astype(jnp.bfloat16)
            precond = jnp.dot(middle, right_root, preferred_element_type=jnp.float32)
            as_float = grad_block.astype(jnp.float32)
            graft_scale = jnp.sqrt(jnp.mean(as_float * as_float) / (jnp.mean(precond * precond) + EPSILON))
            return (gram_left, gram_right, (precond * graft_scale).astype(jnp.bfloat16))

        def empty_case(unused):
            zero_float = jnp.zeros((BS, BS), jnp.float32)
            return (zero_float, zero_float, jnp.zeros((BS, BS), jnp.bfloat16))
        gram_left, gram_right, owner_update = lax.cond(block_id >= 0, occupied_case, empty_case, 0)
        new_left = DECAY * left_old + (1.0 - DECAY) * gram_left
        new_right = DECAY * right_old + (1.0 - DECAY) * gram_right
        return (new_left, new_right, owner_update)
    stat_left_new, stat_right_new, updates = lax.map(per_owner, (owner_block, stat_left, stat_right, root_left, root_right))
    matches = owner_block[None, :] == jnp.arange(BLOCKS, dtype=jnp.int32)[:, None]
    owner_of = lax.optimization_barrier(jnp.sum(jnp.where(matches, jnp.arange(DEVICES, dtype=jnp.int32)[None, :], 0), axis=1)).astype(jnp.int32)
    gathered = jnp.take(updates, owner_of, axis=0)
    update = gathered.reshape(ROW_GROUPS, columns, BS, BS).transpose(0, 2, 1, 3).reshape(ROW_GROUPS, BS, D)
    return (stat_left_new, stat_right_new, update)
```

```python
import functools

import jax
import jax.numpy as jnp
from jax import lax
from jax.experimental import pallas as pl
from jax.experimental.pallas import tpu as pltpu
from jax.sharding import PartitionSpec as P

DECAY = 0.95
EPSILON = 1e-06
MIB = 1 << 20


def params(mib):
    return pltpu.CompilerParams(vmem_limit_bytes=mib * MIB)


def pack_kernel(strips, grads, out, sem, *, half, groups, columns, reps, width):
    copies = []
    for which in range(2):
        for column in range(columns):
            offset = pl.multiple_of((column * reps + strips[which]) * width, width)
            copies.append(
                pltpu.make_async_copy(
                    grads.at[0, pl.ds(half * groups, groups), :, pl.ds(offset, width)],
                    out.at[which, column],
                    sem.at[which * columns + column],
                )
            )
    for copy in copies:
        copy.start()
    for copy in copies:
        copy.wait()


def pack(grads, strips, half, columns, width):
    reps, groups = 4, grads.shape[1] // 2
    return pl.pallas_call(
        functools.partial(pack_kernel, half=half, groups=groups, columns=columns, reps=reps, width=width),
        out_shape=jax.ShapeDtypeStruct((2, columns, groups, grads.shape[2], width), grads.dtype),
        in_specs=[pl.BlockSpec(memory_space=pltpu.SMEM), pl.BlockSpec(memory_space=pl.ANY)],
        out_specs=pl.BlockSpec(memory_space=pl.ANY),
        scratch_shapes=[pltpu.SemaphoreType.DMA((2 * columns,))],
        compiler_params=params(16),
        name="pack",
    )(strips, grads)


def first_sum_kernel(strips, own, passing, received, kept, sending):
    del strips
    kept[0] = (own[0].astype(jnp.float32) + received[0, 0].astype(jnp.float32)).astype(kept.dtype)
    sending[0] = (passing[0].astype(jnp.float32) + received[1, 0].astype(jnp.float32)).astype(sending.dtype)


def first_sum(grads, received, strips, half):
    _, columns, groups, height, width = received.shape
    reps = 4
    piece = (1, groups, height, width)
    result = jax.ShapeDtypeStruct((columns, groups, height, width), received.dtype)
    return pl.pallas_call(
        first_sum_kernel,
        grid_spec=pltpu.PrefetchScalarGridSpec(
            num_scalar_prefetch=1,
            grid=(columns,),
            in_specs=[
                pl.BlockSpec(piece, lambda c, s: (0, half, 0, c * reps + s[0])),
                pl.BlockSpec(piece, lambda c, s: (0, half, 0, c * reps + s[1])),
                pl.BlockSpec((2,) + piece, lambda c, s: (0, c, 0, 0, 0)),
            ],
            out_specs=[pl.BlockSpec(piece, lambda c, s: (c, 0, 0, 0))] * 2,
        ),
        out_shape=[result, result],
        compiler_params=params(16),
        name="first_sum",
    )(strips, grads, grads, received)


def second_sum_kernel(owners, kept_0, received_0, kept_1, received_1, out, *, columns, groups):
    out[...] = jnp.zeros_like(out)
    for half, (kept, received) in enumerate(((kept_0, received_0), (kept_1, received_1))):
        for group in range(groups):
            for column in range(columns):
                owner = owners[(half * groups + group) * columns + column]
                total = kept[column, group].astype(jnp.float32) + received[column, group].astype(jnp.float32)
                out[owner] = total.astype(out.dtype)


def second_sum(owners, kept, received, devices):
    columns, groups, height, width = kept[0].shape
    return pl.pallas_call(
        functools.partial(second_sum_kernel, columns=columns, groups=groups),
        out_shape=jax.ShapeDtypeStruct((devices, height, width), kept[0].dtype),
        in_specs=[pl.BlockSpec(memory_space=pltpu.SMEM)] + [pl.BlockSpec(memory_space=pltpu.VMEM)] * 4,
        out_specs=pl.BlockSpec(memory_space=pltpu.VMEM),
        compiler_params=params(16),
        name="second_sum",
    )(owners, kept[0], received[0], kept[1], received[1])


def update_kernel(left, grad, right, out, precond, square, *, tiles):
    step = pl.program_id(0)
    strips, size, _ = grad.shape
    rows = size // tiles

    @pl.when(step == 0)
    def _():
        square[...] = jnp.zeros_like(square)

    middle = jnp.concatenate(
        [
            jnp.dot(left[0], grad[strip], preferred_element_type=jnp.float32).astype(jnp.bfloat16)
            for strip in range(strips)
        ],
        axis=1,
    )
    part = jnp.dot(middle, right[0], preferred_element_type=jnp.float32)
    precond[pl.ds(pl.multiple_of(step * rows, rows), rows), :] = part
    square[...] += jnp.sum((part * part).reshape(rows // 8, 8, size), axis=0)

    @pl.when(step == tiles - 1)
    def _():
        grad_square = jnp.zeros((8, grad.shape[2]), jnp.float32)
        for strip in range(strips):
            as_float = grad[strip].astype(jnp.float32)
            grad_square += jnp.sum((as_float * as_float).reshape(size // 8, 8, -1), axis=0)
        entries = size * size
        mean_grad = jnp.sum(grad_square) / entries
        mean_precond = jnp.sum(square[...]) / entries
        scale = jnp.sqrt(jnp.full((8, 128), mean_grad) / (jnp.full((8, 128), mean_precond) + EPSILON))
        out[...] = (precond[...] * scale[0:1, 0:1]).astype(out.dtype)


def block_update(left, grad, right, tiles=2):
    strips, size, width = grad.shape
    rows = size // tiles
    return pl.pallas_call(
        functools.partial(update_kernel, tiles=tiles),
        grid=(tiles,),
        out_shape=jax.ShapeDtypeStruct((size, size), jnp.bfloat16),
        in_specs=[
            pl.BlockSpec((1, rows, size), lambda t: (0, t, 0)),
            pl.BlockSpec((strips, size, width), lambda t: (0, 0, 0)),
            pl.BlockSpec((1, size, size), lambda t: (0, 0, 0)),
        ],
        out_specs=pl.BlockSpec((size, size), lambda t: (0, 0)),
        scratch_shapes=[pltpu.VMEM((size, size), jnp.float32), pltpu.VMEM((8, size), jnp.float32)],
        compiler_params=params(32),
        cost_estimate=pl.CostEstimate(flops=4 * size**3, bytes_accessed=8 * size * size, transcendentals=0),
        name="block_update",
    )(left, grad, right)


def statistics_kernel(grad, left, right, new_left, new_right):
    step = pl.program_id(0)
    strips, size, width = grad.shape
    rows = pl.ds(pl.multiple_of(step * width, width), width)
    gram = jnp.zeros((width, size), jnp.float32)
    for strip in range(strips):
        gram += lax.dot_general(
            grad[strip, rows, :], grad[strip], (((1,), (1,)), ((), ())), preferred_element_type=jnp.float32
        )
    new_left[0] = DECAY * left[0] + (1.0 - DECAY) * gram
    for strip in range(strips):
        columns = slice(strip * width, (strip + 1) * width)
        gram = lax.dot_general(
            grad[step], grad[strip], (((0,), (0,)), ((), ())), preferred_element_type=jnp.float32
        )
        new_right[0, :, columns] = DECAY * right[0, :, columns] + (1.0 - DECAY) * gram


def statistics(grad, left, right):
    strips, size, width = grad.shape
    rows = pl.BlockSpec((1, width, size), lambda t: (0, t, 0))
    return pl.pallas_call(
        statistics_kernel,
        grid=(strips,),
        out_shape=[jax.ShapeDtypeStruct(left.shape, left.dtype)] * 2,
        in_specs=[pl.BlockSpec((strips, size, width), lambda t: (0, 0, 0)), rows, rows],
        out_specs=[rows, rows],
        compiler_params=params(32),
        cost_estimate=pl.CostEstimate(flops=4 * size**3, bytes_accessed=18 * size * size, transcendentals=0),
        name="statistics",
    )(grad, left, right)


def pick_kernel(owners, returned, out, sem, *, columns, size):
    groups = out.shape[0]
    copies = []
    for group in range(groups):
        for column in range(columns):
            block = group * columns + column
            copies.append(
                pltpu.make_async_copy(
                    returned.at[owners[block]],
                    out.at[group, :, pl.ds(column * size, size)],
                    sem.at[block],
                )
            )
    for copy in copies:
        copy.start()
    for copy in copies:
        copy.wait()


def pick(owners, returned, groups, columns):
    _, rows, size = returned.shape
    return pl.pallas_call(
        functools.partial(pick_kernel, columns=columns, size=size),
        out_shape=jax.ShapeDtypeStruct((groups, rows, columns * size), returned.dtype),
        in_specs=[pl.BlockSpec(memory_space=pltpu.SMEM), pl.BlockSpec(memory_space=pl.ANY)],
        out_specs=pl.BlockSpec(memory_space=pl.ANY),
        scratch_shapes=[pltpu.SemaphoreType.DMA((groups * columns,))],
        compiler_params=params(16),
        name="pick",
    )(owners, returned)


def body(grads, stat_left, stat_right, root_left, root_right, owner_block):
    reps = lax.axis_size("rep")
    devices = lax.axis_size("fsdp") * reps
    size = stat_left.shape[1]
    groups, full_width = grads.shape[1], grads.shape[3]
    columns = full_width // size
    width = size // reps
    me = lax.axis_index("rep")
    across = [(r, r ^ 1) for r in range(reps)]
    mirror = [(r, reps - 1 - r) for r in range(reps)]
    orders = ((across, mirror), (mirror, across))
    firsts = (me ^ 1, reps - 1 - me)

    matches = owner_block[None, :] == lax.iota(jnp.int32, groups * columns)[:, None]
    owners = jnp.sum(jnp.where(matches, lax.iota(jnp.int32, devices)[None, :], 0), axis=1)

    kept, received = [], []
    arrived = []
    for half in range(2):
        partner = firsts[half]
        partner_second = (reps - 1 - partner, partner ^ 1)[half]
        packed = pack(grads, jnp.stack([partner, partner_second]).astype(jnp.int32), half, columns, width)
        arrived.append(lax.ppermute(packed, "rep", orders[half][0]))
    for half in range(2):
        own_second = (reps - 1 - me, me ^ 1)[half]
        keep, sending = first_sum(grads, arrived[half], jnp.stack([me, own_second]).astype(jnp.int32), half)
        kept.append(keep)
        received.append(lax.ppermute(sending, "rep", orders[half][1]))
    pieces = second_sum(owners, kept, received, devices)
    grad_block = lax.all_to_all(pieces, ("rep", "fsdp"), split_axis=0, concat_axis=0, tiled=True)
    grad_block = grad_block.reshape(reps, size, width)
    update_block = block_update(root_left, grad_block, root_right)
    returned = lax.all_to_all(
        update_block.reshape(devices, size // devices, size),
        ("rep", "fsdp"),
        split_axis=0,
        concat_axis=0,
        tiled=True,
    )
    new_left, new_right = statistics(grad_block, stat_left, stat_right)
    return (new_left, new_right, pick(owners, returned, groups, columns))


def solution(mesh):
    in_specs = (
        P("rep", None, "fsdp", None),
        P(("rep", "fsdp"), None, None),
        P(("rep", "fsdp"), None, None),
        P(("rep", "fsdp"), None, None),
        P(("rep", "fsdp"), None, None),
        P(),
    )
    out_specs = (
        P(("rep", "fsdp"), None, None),
        P(("rep", "fsdp"), None, None),
        P(None, ("rep", "fsdp"), None),
    )
    return jax.shard_map(body, mesh=mesh, in_specs=in_specs, out_specs=out_specs, check_vma=False)
```

```python
import functools

import jax
import jax.numpy as jnp
from jax import lax
from jax.experimental import pallas as pl
from jax.experimental.pallas import tpu as pltpu
from jax.sharding import PartitionSpec as P

DECAY = 0.95
EPSILON = 1e-06
MIB = 1 << 20


def params(mib):
    return pltpu.CompilerParams(vmem_limit_bytes=mib * MIB)


def first_partner(part, me, reps):
    return (me ^ 1, reps - 1 - me)[part % 2]


def second_partner(part, me, reps):
    return (reps - 1 - me, me ^ 1)[part % 2]


def pack_kernel(grads, *rest, parts, own, groups, columns, reps, width):
    outs, sem = rest[:-1], rest[-1]
    me = lax.axis_index("rep")
    copies = []
    for out, part in zip(outs, parts):
        target = me if own else first_partner(part, me, reps)
        for which, strip in enumerate((target, second_partner(part, target, reps))):
            for column in range(columns):
                offset = pl.multiple_of((column * reps + strip) * width, width)
                copies.append(
                    pltpu.make_async_copy(
                        grads.at[0, pl.ds(part * groups, groups), :, pl.ds(offset, width)],
                        out.at[which, column],
                        sem.at[len(copies)],
                    )
                )
    for copy in copies:
        copy.start()
    for copy in copies:
        copy.wait()


def pack(grads, parts, own, groups, columns, reps, width):
    shape = jax.ShapeDtypeStruct((2, columns, groups, grads.shape[2], width), grads.dtype)
    return pl.pallas_call(
        functools.partial(
            pack_kernel, parts=parts, own=own, groups=groups, columns=columns, reps=reps, width=width
        ),
        out_shape=[shape] * len(parts),
        in_specs=[pl.BlockSpec(memory_space=pltpu.HBM)],
        out_specs=[pl.BlockSpec(memory_space=pl.ANY)] * len(parts),
        scratch_shapes=[pltpu.SemaphoreType.DMA((2 * columns * len(parts),))],
        compiler_params=params(16),
        name="pack_own" if own else "pack",
    )(pltpu.with_memory_space_constraint(grads, pltpu.HBM))


def first_sum_kernel(own, received, sending):
    _, columns, groups, _, _ = own.shape
    for column in range(columns):
        for group in range(groups):
            total = own[1, column, group].astype(jnp.float32) + received[1, column, group].astype(jnp.float32)
            sending[column, group] = total.astype(sending.dtype)


def first_sum(own, received):
    return pl.pallas_call(
        first_sum_kernel,
        out_shape=jax.ShapeDtypeStruct(own.shape[1:], own.dtype),
        in_specs=[pl.BlockSpec(memory_space=pltpu.VMEM)] * 2,
        out_specs=pl.BlockSpec(memory_space=pltpu.VMEM),
        compiler_params=params(16),
        name="first_sum",
    )(own, received)


def second_sum_kernel(owners, *refs, parts, columns, groups, initial):
    out = refs[-1]
    if initial:
        out[...] = jnp.zeros_like(out)
    for index, part in enumerate(parts):
        own, first, second = refs[3 * index : 3 * index + 3]
        for group in range(groups):
            for column in range(columns):
                owner = owners[(part * groups + group) * columns + column]
                total = own[0, column, group].astype(jnp.float32) + first[0, column, group].astype(jnp.float32)
                total += second[column, group].astype(jnp.float32)
                out[owner] = total.astype(out.dtype)


def second_sum(owners, terms, parts, devices, before=None):
    _, columns, groups, height, width = terms[0][0].shape
    arrays = [array for part in parts for array in terms[part]]
    aliases = {}
    if before is not None:
        arrays.append(before)
        aliases = {len(arrays): 0}
    return pl.pallas_call(
        functools.partial(
            second_sum_kernel, parts=parts, columns=columns, groups=groups, initial=before is None
        ),
        out_shape=jax.ShapeDtypeStruct((devices, height, width), arrays[0].dtype),
        in_specs=[pl.BlockSpec(memory_space=pltpu.SMEM)] + [pl.BlockSpec(memory_space=pltpu.VMEM)] * len(arrays),
        out_specs=pl.BlockSpec(memory_space=pltpu.VMEM),
        input_output_aliases=aliases,
        compiler_params=params(16),
        name="second_sum",
    )(owners, *arrays)


def update_kernel(left, grad, right, out, precond, scaled, sem, *, tiles, out_tiles):
    strips, size, width = grad.shape
    rows = size // tiles
    grad_square = jnp.zeros((8, width), jnp.float32)
    square = jnp.zeros((8, size), jnp.float32)
    for tile in range(tiles):
        band = slice(tile * rows, (tile + 1) * rows)
        middle = jnp.concatenate(
            [
                jnp.dot(left[0, band, :], grad[strip], preferred_element_type=jnp.float32).astype(jnp.bfloat16)
                for strip in range(strips)
            ],
            axis=1,
        )
        for strip in range(tile * strips // tiles, (tile + 1) * strips // tiles):
            as_float = grad[strip].astype(jnp.float32)
            grad_square += jnp.sum((as_float * as_float).reshape(size // 8, 8, width), axis=0)
        part = jnp.dot(middle, right[0], preferred_element_type=jnp.float32)
        precond[band, :] = part
        square += jnp.sum((part * part).reshape(rows // 8, 8, size), axis=0)
    entries = size * size
    mean_grad = jnp.full((8, 128), jnp.sum(grad_square) / entries)
    mean_precond = jnp.full((8, 128), jnp.sum(square) / entries)
    scale = jnp.sqrt(mean_grad / (mean_precond + EPSILON))[0:1, 0:1]
    out_rows = size // out_tiles
    copies = []
    for tile in range(out_tiles):
        band = slice(tile * out_rows, (tile + 1) * out_rows)
        scaled[band, :] = (precond[band, :] * scale).astype(out.dtype)
        copies.append(pltpu.make_async_copy(scaled.at[band, :], out.at[band, :], sem.at[tile]))
        copies[-1].start()
    for copy in copies:
        copy.wait()


def block_update(left, grad, right, tiles=2, out_tiles=4):
    strips, size, width = grad.shape
    return pl.pallas_call(
        functools.partial(update_kernel, tiles=tiles, out_tiles=out_tiles),
        out_shape=pltpu.HBM((size, size), jnp.bfloat16),
        in_specs=[pl.BlockSpec(memory_space=pltpu.VMEM)] * 3,
        out_specs=pl.BlockSpec(memory_space=pltpu.HBM),
        scratch_shapes=[
            pltpu.VMEM((size, size), jnp.float32),
            pltpu.VMEM((size, size), jnp.bfloat16),
            pltpu.SemaphoreType.DMA((out_tiles,)),
        ],
        compiler_params=params(32),
        cost_estimate=pl.CostEstimate(flops=4 * size**3, bytes_accessed=8 * size * size, transcendentals=0),
        name="block_update",
    )(left, grad, right)


def statistics_kernel(grad, left, right, new_left, new_right):
    step = pl.program_id(0)
    strips, size, width = grad.shape
    rows = pl.ds(pl.multiple_of(step * width, width), width)
    gram = jnp.zeros((width, size), jnp.float32)
    for strip in range(strips):
        gram += lax.dot_general(
            grad[strip, rows, :], grad[strip], (((1,), (1,)), ((), ())), preferred_element_type=jnp.float32
        )
    new_left[0] = DECAY * left[0] + (1.0 - DECAY) * gram
    for strip in range(strips):
        columns = slice(strip * width, (strip + 1) * width)
        gram = lax.dot_general(
            grad[step], grad[strip], (((0,), (0,)), ((), ())), preferred_element_type=jnp.float32
        )
        new_right[0, :, columns] = DECAY * right[0, :, columns] + (1.0 - DECAY) * gram


def statistics(grad, left, right):
    strips, size, width = grad.shape
    rows = pl.BlockSpec((1, width, size), lambda t: (0, t, 0))
    return pl.pallas_call(
        statistics_kernel,
        grid=(strips,),
        out_shape=[jax.ShapeDtypeStruct(left.shape, left.dtype)] * 2,
        in_specs=[pl.BlockSpec((strips, size, width), lambda t: (0, 0, 0)), rows, rows],
        out_specs=[rows, rows],
        compiler_params=params(32),
        cost_estimate=pl.CostEstimate(flops=4 * size**3, bytes_accessed=18 * size * size, transcendentals=0),
        name="statistics",
    )(grad, left, right)


def pick_kernel(owners, returned, out, sem, *, columns, size):
    groups = out.shape[0]
    copies = []
    for group in range(groups):
        for column in range(columns):
            block = group * columns + column
            copies.append(
                pltpu.make_async_copy(
                    returned.at[owners[block]],
                    out.at[group, :, pl.ds(column * size, size)],
                    sem.at[block],
                )
            )
    for copy in copies:
        copy.start()
    for copy in copies:
        copy.wait()


def pick(owners, returned, groups, columns):
    _, rows, size = returned.shape
    return pl.pallas_call(
        functools.partial(pick_kernel, columns=columns, size=size),
        out_shape=jax.ShapeDtypeStruct((groups, rows, columns * size), returned.dtype),
        in_specs=[pl.BlockSpec(memory_space=pltpu.SMEM), pl.BlockSpec(memory_space=pl.ANY)],
        out_specs=pl.BlockSpec(memory_space=pl.ANY),
        scratch_shapes=[pltpu.SemaphoreType.DMA((groups * columns,))],
        compiler_params=params(16),
        name="pick",
    )(owners, returned)


def body(grads, stat_left, stat_right, root_left, root_right, owner_block):
    reps = lax.axis_size("rep")
    devices = lax.axis_size("fsdp") * reps
    size = stat_left.shape[1]
    groups, full_width = grads.shape[1], grads.shape[3]
    columns = full_width // size
    width = size // reps
    across = [(r, r ^ 1) for r in range(reps)]
    mirror = [(r, reps - 1 - r) for r in range(reps)]
    orders = ((across, mirror), (mirror, across))

    matches = owner_block[None, :] == lax.iota(jnp.int32, groups * columns)[:, None]
    owners = jnp.sum(jnp.where(matches, lax.iota(jnp.int32, devices)[None, :], 0), axis=1)

    parts = 4
    part_groups = groups // parts
    sizes = (part_groups, columns, reps, width)
    packed = pack(grads, (0, 1), False, *sizes) + pack(grads, (2, 3), False, *sizes)
    firsts = [lax.ppermute(packed[part], "rep", orders[part % 2][0]) for part in range(parts)]
    own = pack(grads, tuple(range(parts)), True, *sizes)
    seconds = [
        lax.ppermute(first_sum(own[part], firsts[part]), "rep", orders[part % 2][1]) for part in range(parts)
    ]
    terms = list(zip(own, firsts, seconds))
    pieces = second_sum(owners, terms, (0, 1), devices)
    pieces = second_sum(owners, terms, (2, 3), devices, pieces)
    grad_block = lax.all_to_all(pieces, ("rep", "fsdp"), split_axis=0, concat_axis=0, tiled=True)
    grad_block = grad_block.reshape(reps, size, width)
    update_block = block_update(root_left, grad_block, root_right)
    returned = lax.all_to_all(
        update_block.reshape(devices, size // devices, size),
        ("rep", "fsdp"),
        split_axis=0,
        concat_axis=0,
        tiled=True,
    )
    new_left, new_right = statistics(grad_block, stat_left, stat_right)
    return (new_left, new_right, pick(owners, returned, groups, columns))


def solution(mesh):
    in_specs = (
        P("rep", None, "fsdp", None),
        P(("rep", "fsdp"), None, None),
        P(("rep", "fsdp"), None, None),
        P(("rep", "fsdp"), None, None),
        P(("rep", "fsdp"), None, None),
        P(),
    )
    out_specs = (
        P(("rep", "fsdp"), None, None),
        P(("rep", "fsdp"), None, None),
        P(None, ("rep", "fsdp"), None),
    )
    return jax.shard_map(body, mesh=mesh, in_specs=in_specs, out_specs=out_specs, check_vma=False)
```

```python
import functools

import jax
import jax.numpy as jnp
from jax import lax
from jax.experimental import pallas as pl
from jax.experimental.pallas import tpu as pltpu
from jax.sharding import PartitionSpec as P

DECAY = 0.95
EPSILON = 1e-06
MIB = 1 << 20
STAGE_GROUPS = (2, 2, 2)


def params(mib):
    return pltpu.CompilerParams(vmem_limit_bytes=mib * MIB)


def first_partner(part, me, reps):
    return (me ^ 1, reps - 1 - me)[part % 2]


def second_partner(part, me, reps):
    return (reps - 1 - me, me ^ 1)[part % 2]


def pack_kernel(grads, *rest, parts, spans, own, columns, reps, width):
    outs, sem = rest[:-1], rest[-1]
    me = lax.axis_index("rep")
    copies = []
    for out, part in zip(outs, parts):
        start, groups = spans[part]
        target = me if own else first_partner(part, me, reps)
        for which, strip in enumerate((target, second_partner(part, target, reps))):
            for column in range(columns):
                offset = pl.multiple_of((column * reps + strip) * width, width)
                copies.append(
                    pltpu.make_async_copy(
                        grads.at[0, pl.ds(start, groups), :, pl.ds(offset, width)],
                        out.at[which, column],
                        sem.at[len(copies)],
                    )
                )
    for copy in copies:
        copy.start()
    for copy in copies:
        copy.wait()


def pack(grads, parts, spans, own, columns, reps, width):
    return pl.pallas_call(
        functools.partial(
            pack_kernel, parts=parts, spans=spans, own=own, columns=columns, reps=reps, width=width
        ),
        out_shape=[
            jax.ShapeDtypeStruct((2, columns, spans[part][1], grads.shape[2], width), grads.dtype) for part in parts
        ],
        in_specs=[pl.BlockSpec(memory_space=pltpu.HBM)],
        out_specs=[pl.BlockSpec(memory_space=pl.ANY)] * len(parts),
        scratch_shapes=[pltpu.SemaphoreType.DMA((2 * columns * len(parts),))],
        compiler_params=params(16),
        name="pack_own" if own else "pack",
    )(pltpu.with_memory_space_constraint(grads, pltpu.HBM))


def first_sum_kernel(own, received, sending):
    _, columns, groups, _, _ = own.shape
    for column in range(columns):
        for group in range(groups):
            total = own[1, column, group].astype(jnp.float32) + received[1, column, group].astype(jnp.float32)
            sending[column, group] = total.astype(sending.dtype)


def first_sum(own, received):
    return pl.pallas_call(
        first_sum_kernel,
        out_shape=jax.ShapeDtypeStruct(own.shape[1:], own.dtype),
        in_specs=[pl.BlockSpec(memory_space=pltpu.VMEM)] * 2,
        out_specs=pl.BlockSpec(memory_space=pltpu.VMEM),
        compiler_params=params(16),
        name="first_sum",
    )(own, received)


def second_sum_kernel(owners, *refs, parts, spans, columns, initial):
    out = refs[-1]
    if initial:
        out[...] = jnp.zeros_like(out)
    for index, part in enumerate(parts):
        own, first, second = refs[3 * index : 3 * index + 3]
        start, groups = spans[part]
        for group in range(groups):
            for column in range(columns):
                owner = owners[(start + group) * columns + column]
                total = own[0, column, group].astype(jnp.float32) + first[0, column, group].astype(jnp.float32)
                total += second[column, group].astype(jnp.float32)
                out[owner] = total.astype(out.dtype)


def second_sum(owners, terms, parts, spans, devices, before=None):
    _, columns, _, height, width = terms[0][0].shape
    arrays = [array for part in parts for array in terms[part]]
    aliases = {}
    if before is not None:
        arrays.append(before)
        aliases = {len(arrays): 0}
    return pl.pallas_call(
        functools.partial(
            second_sum_kernel, parts=parts, spans=spans, columns=columns, initial=before is None
        ),
        out_shape=jax.ShapeDtypeStruct((devices, height, width), arrays[0].dtype),
        in_specs=[pl.BlockSpec(memory_space=pltpu.SMEM)] + [pl.BlockSpec(memory_space=pltpu.VMEM)] * len(arrays),
        out_specs=pl.BlockSpec(memory_space=pltpu.VMEM),
        input_output_aliases=aliases,
        compiler_params=params(16),
        name="second_sum",
    )(owners, *arrays)


def update_kernel(left, grad, right, out, precond, scaled, sem, *, tiles, out_tiles):
    strips, size, width = grad.shape
    rows = size // tiles
    grad_square = jnp.zeros((8, width), jnp.float32)
    square = jnp.zeros((8, size), jnp.float32)
    for tile in range(tiles):
        band = slice(tile * rows, (tile + 1) * rows)
        middle = jnp.concatenate(
            [
                jnp.dot(left[0, band, :], grad[strip], preferred_element_type=jnp.float32).astype(jnp.bfloat16)
                for strip in range(strips)
            ],
            axis=1,
        )
        for strip in range(tile * strips // tiles, (tile + 1) * strips // tiles):
            as_float = grad[strip].astype(jnp.float32)
            grad_square += jnp.sum((as_float * as_float).reshape(size // 8, 8, width), axis=0)
        part = jnp.dot(middle, right[0], preferred_element_type=jnp.float32)
        precond[band, :] = part
        square += jnp.sum((part * part).reshape(rows // 8, 8, size), axis=0)
    entries = size * size
    mean_grad = jnp.full((8, 128), jnp.sum(grad_square) / entries)
    mean_precond = jnp.full((8, 128), jnp.sum(square) / entries)
    scale = jnp.sqrt(mean_grad / (mean_precond + EPSILON))[0:1, 0:1]
    out_rows = size // out_tiles
    copies = []
    for tile in range(out_tiles):
        band = slice(tile * out_rows, (tile + 1) * out_rows)
        scaled[band, :] = (precond[band, :] * scale).astype(out.dtype)
        copies.append(pltpu.make_async_copy(scaled.at[band, :], out.at[band, :], sem.at[tile]))
        copies[-1].start()
    for copy in copies:
        copy.wait()


def block_update(left, grad, right, tiles=2, out_tiles=4):
    strips, size, width = grad.shape
    return pl.pallas_call(
        functools.partial(update_kernel, tiles=tiles, out_tiles=out_tiles),
        out_shape=pltpu.HBM((size, size), jnp.bfloat16),
        in_specs=[pl.BlockSpec(memory_space=pltpu.VMEM)] * 3,
        out_specs=pl.BlockSpec(memory_space=pltpu.HBM),
        scratch_shapes=[
            pltpu.VMEM((size, size), jnp.float32),
            pltpu.VMEM((size, size), jnp.bfloat16),
            pltpu.SemaphoreType.DMA((out_tiles,)),
        ],
        compiler_params=params(32),
        cost_estimate=pl.CostEstimate(flops=4 * size**3, bytes_accessed=8 * size * size, transcendentals=0),
        name="block_update",
    )(left, grad, right)


def statistics_kernel(grad, left, right, new_left, new_right):
    step = pl.program_id(0)
    strips, size, width = grad.shape
    rows = pl.ds(pl.multiple_of(step * width, width), width)
    gram = jnp.zeros((width, size), jnp.float32)
    for strip in range(strips):
        gram += lax.dot_general(
            grad[strip, rows, :], grad[strip], (((1,), (1,)), ((), ())), preferred_element_type=jnp.float32
        )
    new_left[0] = DECAY * left[0] + (1.0 - DECAY) * gram
    for strip in range(strips):
        columns = slice(strip * width, (strip + 1) * width)
        gram = lax.dot_general(
            grad[step], grad[strip], (((0,), (0,)), ((), ())), preferred_element_type=jnp.float32
        )
        new_right[0, :, columns] = DECAY * right[0, :, columns] + (1.0 - DECAY) * gram


def statistics(grad, left, right):
    strips, size, width = grad.shape
    rows = pl.BlockSpec((1, width, size), lambda t: (0, t, 0))
    return pl.pallas_call(
        statistics_kernel,
        grid=(strips,),
        out_shape=[jax.ShapeDtypeStruct(left.shape, left.dtype)] * 2,
        in_specs=[pl.BlockSpec((strips, size, width), lambda t: (0, 0, 0)), rows, rows],
        out_specs=[rows, rows],
        compiler_params=params(32),
        cost_estimate=pl.CostEstimate(flops=4 * size**3, bytes_accessed=18 * size * size, transcendentals=0),
        name="statistics",
    )(grad, left, right)


def pick_kernel(owners, returned, out, gathered, sem, *, columns, size, steps):
    groups = out.shape[0] // steps
    copies = []
    for step in range(steps):
        band = pl.ds(step * groups, groups)
        for group in range(step * groups, (step + 1) * groups):
            for column in range(columns):
                piece = returned[owners[group * columns + column]]
                gathered[group, :, column * size : (column + 1) * size] = piece
        copies.append(pltpu.make_async_copy(gathered.at[band], out.at[band], sem.at[step]))
        copies[-1].start()
    for copy in copies:
        copy.wait()


def pick(owners, returned, groups, columns, steps=6):
    _, rows, size = returned.shape
    shape = (groups, rows, columns * size)
    return pl.pallas_call(
        functools.partial(pick_kernel, columns=columns, size=size, steps=steps),
        out_shape=pltpu.HBM(shape, returned.dtype),
        in_specs=[pl.BlockSpec(memory_space=pltpu.SMEM), pl.BlockSpec(memory_space=pltpu.VMEM)],
        out_specs=pl.BlockSpec(memory_space=pltpu.HBM),
        scratch_shapes=[pltpu.VMEM(shape, returned.dtype), pltpu.SemaphoreType.DMA((steps,))],
        compiler_params=params(16),
        name="pick",
    )(owners, returned)


def body(grads, stat_left, stat_right, root_left, root_right, owner_block):
    reps = lax.axis_size("rep")
    devices = lax.axis_size("fsdp") * reps
    size = stat_left.shape[1]
    groups, full_width = grads.shape[1], grads.shape[3]
    columns = full_width // size
    width = size // reps
    across = [(r, r ^ 1) for r in range(reps)]
    mirror = [(r, reps - 1 - r) for r in range(reps)]
    orders = ((across, mirror), (mirror, across))

    matches = owner_block[None, :] == lax.iota(jnp.int32, groups * columns)[:, None]
    owners = jnp.sum(jnp.where(matches, lax.iota(jnp.int32, devices)[None, :], 0), axis=1)

    stages = len(STAGE_GROUPS)
    spans, start = [], 0
    for count in STAGE_GROUPS:
        for _ in range(2):
            spans.append((start, count))
            start += count
    parts = range(2 * stages)
    pairs = [(2 * stage, 2 * stage + 1) for stage in range(stages)]
    sizes = (columns, reps, width)
    packed = [part for pair in pairs for part in pack(grads, pair, spans, False, *sizes)]
    firsts = [lax.ppermute(packed[part], "rep", orders[part % 2][0]) for part in parts]
    own = pack(grads, tuple(parts), spans, True, *sizes)
    seconds = [
        lax.ppermute(first_sum(own[part], firsts[part]), "rep", orders[part % 2][1]) for part in parts
    ]
    terms = list(zip(own, firsts, seconds))
    pieces = None
    for pair in pairs:
        pieces = second_sum(owners, terms, pair, spans, devices, pieces)
    grad_block = lax.all_to_all(pieces, ("rep", "fsdp"), split_axis=0, concat_axis=0, tiled=True)
    grad_block = grad_block.reshape(reps, size, width)
    update_block = block_update(root_left, grad_block, root_right)
    returned = lax.all_to_all(
        update_block.reshape(devices, size // devices, size),
        ("rep", "fsdp"),
        split_axis=0,
        concat_axis=0,
        tiled=True,
    )
    new_left, new_right = statistics(grad_block, stat_left, stat_right)
    return (new_left, new_right, pick(owners, returned, groups, columns))


def solution(mesh):
    in_specs = (
        P("rep", None, "fsdp", None),
        P(("rep", "fsdp"), None, None),
        P(("rep", "fsdp"), None, None),
        P(("rep", "fsdp"), None, None),
        P(("rep", "fsdp"), None, None),
        P(),
    )
    out_specs = (
        P(("rep", "fsdp"), None, None),
        P(("rep", "fsdp"), None, None),
        P(None, ("rep", "fsdp"), None),
    )
    return jax.shard_map(body, mesh=mesh, in_specs=in_specs, out_specs=out_specs, check_vma=False)
```

```python
import functools

import jax
import jax.numpy as jnp
from jax import lax
from jax.experimental import pallas as pl
from jax.experimental.pallas import tpu as pltpu
from jax.sharding import PartitionSpec as P

DECAY = 0.95
EPSILON = 1e-06
MIB = 1 << 20
STAGE_GROUPS = (2, 2, 2)


def params(mib):
    return pltpu.CompilerParams(vmem_limit_bytes=mib * MIB)


def first_partner(part, me, reps):
    return (me ^ 1, reps - 1 - me)[part % 2]


def second_partner(part, me, reps):
    return (reps - 1 - me, me ^ 1)[part % 2]


def pack_kernel(grads, *rest, parts, spans, own, columns, reps, width):
    outs, sem = rest[:-1], rest[-1]
    me = lax.axis_index("rep")
    copies = []
    for out, part in zip(outs, parts):
        start, groups = spans[part]
        target = me if own else first_partner(part, me, reps)
        for which, strip in enumerate((target, second_partner(part, target, reps))):
            for column in range(columns):
                offset = pl.multiple_of((column * reps + strip) * width, width)
                copies.append(
                    pltpu.make_async_copy(
                        grads.at[0, pl.ds(start, groups), :, pl.ds(offset, width)],
                        out.at[which, column],
                        sem.at[len(copies)],
                    )
                )
    for copy in copies:
        copy.start()
    for copy in copies:
        copy.wait()


def pack(grads, parts, spans, own, columns, reps, width):
    return pl.pallas_call(
        functools.partial(
            pack_kernel, parts=parts, spans=spans, own=own, columns=columns, reps=reps, width=width
        ),
        out_shape=[
            jax.ShapeDtypeStruct((2, columns, spans[part][1], grads.shape[2], width), grads.dtype) for part in parts
        ],
        in_specs=[pl.BlockSpec(memory_space=pltpu.HBM)],
        out_specs=[pl.BlockSpec(memory_space=pl.ANY)] * len(parts),
        scratch_shapes=[pltpu.SemaphoreType.DMA((2 * columns * len(parts),))],
        compiler_params=params(16),
        name="pack_own" if own else "pack",
    )(pltpu.with_memory_space_constraint(grads, pltpu.HBM))


def first_sum_kernel(own, received, sending):
    _, columns, groups, _, _ = own.shape
    for column in range(columns):
        for group in range(groups):
            total = own[1, column, group].astype(jnp.float32) + received[1, column, group].astype(jnp.float32)
            sending[column, group] = total.astype(sending.dtype)


def first_sum(own, received):
    return pl.pallas_call(
        first_sum_kernel,
        out_shape=jax.ShapeDtypeStruct(own.shape[1:], own.dtype),
        in_specs=[pl.BlockSpec(memory_space=pltpu.VMEM)] * 2,
        out_specs=pl.BlockSpec(memory_space=pltpu.VMEM),
        compiler_params=params(16),
        name="first_sum",
    )(own, received)


def second_sum_kernel(owners, *refs, parts, spans, columns, initial):
    out = refs[-1]
    if initial:
        out[...] = jnp.zeros_like(out)
    for index, part in enumerate(parts):
        own, first, second = refs[3 * index : 3 * index + 3]
        start, groups = spans[part]
        for group in range(groups):
            for column in range(columns):
                owner = owners[(start + group) * columns + column]
                total = own[0, column, group].astype(jnp.float32) + first[0, column, group].astype(jnp.float32)
                total += second[column, group].astype(jnp.float32)
                out[owner] = total.astype(out.dtype)


def second_sum(owners, terms, parts, spans, devices, before=None):
    _, columns, _, height, width = terms[0][0].shape
    arrays = [array for part in parts for array in terms[part]]
    aliases = {}
    if before is not None:
        arrays.append(before)
        aliases = {len(arrays): 0}
    return pl.pallas_call(
        functools.partial(
            second_sum_kernel, parts=parts, spans=spans, columns=columns, initial=before is None
        ),
        out_shape=jax.ShapeDtypeStruct((devices, height, width), arrays[0].dtype),
        in_specs=[pl.BlockSpec(memory_space=pltpu.SMEM)] + [pl.BlockSpec(memory_space=pltpu.VMEM)] * len(arrays),
        out_specs=pl.BlockSpec(memory_space=pltpu.VMEM),
        input_output_aliases=aliases,
        compiler_params=params(16),
        name="second_sum",
    )(owners, *arrays)


def update_kernel(left, grad, right, out, precond, scaled, sem, *, tiles, out_tiles):
    strips, size, width = grad.shape
    rows = size // tiles
    grad_square = jnp.zeros((8, width), jnp.float32)
    square = jnp.zeros((8, size), jnp.float32)
    for tile in range(tiles):
        band = slice(tile * rows, (tile + 1) * rows)
        middle = jnp.concatenate(
            [
                jnp.dot(left[0, band, :], grad[strip], preferred_element_type=jnp.float32).astype(jnp.bfloat16)
                for strip in range(strips)
            ],
            axis=1,
        )
        for strip in range(tile * strips // tiles, (tile + 1) * strips // tiles):
            as_float = grad[strip].astype(jnp.float32)
            grad_square += jnp.sum((as_float * as_float).reshape(size // 8, 8, width), axis=0)
        part = jnp.dot(middle, right[0], preferred_element_type=jnp.float32)
        precond[band, :] = part
        square += jnp.sum((part * part).reshape(rows // 8, 8, size), axis=0)
    entries = size * size
    mean_grad = jnp.full((8, 128), jnp.sum(grad_square) / entries)
    mean_precond = jnp.full((8, 128), jnp.sum(square) / entries)
    scale = jnp.sqrt(mean_grad / (mean_precond + EPSILON))[0:1, 0:1]
    eighth = size // (2 * out_tiles)
    edges = [0] + list(range(eighth, size, 2 * eighth)) + [size]
    copies = []
    for tile, (start, end) in enumerate(zip(edges[:-1], edges[1:])):
        band = slice(start, end)
        scaled[band, :] = (precond[band, :] * scale).astype(out.dtype)
        copies.append(pltpu.make_async_copy(scaled.at[band, :], out.at[band, :], sem.at[tile]))
        copies[-1].start()
    for copy in copies:
        copy.wait()


def block_update(left, grad, right, tiles=2, out_tiles=4):
    strips, size, width = grad.shape
    return pl.pallas_call(
        functools.partial(update_kernel, tiles=tiles, out_tiles=out_tiles),
        out_shape=pltpu.HBM((size, size), jnp.bfloat16),
        in_specs=[pl.BlockSpec(memory_space=pltpu.VMEM)] * 3,
        out_specs=pl.BlockSpec(memory_space=pltpu.HBM),
        scratch_shapes=[
            pltpu.VMEM((size, size), jnp.float32),
            pltpu.VMEM((size, size), jnp.bfloat16),
            pltpu.SemaphoreType.DMA((out_tiles + 1,)),
        ],
        compiler_params=params(32),
        cost_estimate=pl.CostEstimate(flops=4 * size**3, bytes_accessed=8 * size * size, transcendentals=0),
        name="block_update",
    )(left, grad, right)


def statistics_kernel(grad, left, right, new_left, new_right):
    step = pl.program_id(0)
    strips, size, width = grad.shape
    rows = pl.ds(pl.multiple_of(step * width, width), width)
    gram = jnp.zeros((width, size), jnp.float32)
    for strip in range(strips):
        gram += lax.dot_general(
            grad[strip, rows, :], grad[strip], (((1,), (1,)), ((), ())), preferred_element_type=jnp.float32
        )
    new_left[0] = DECAY * left[0] + (1.0 - DECAY) * gram
    for strip in range(strips):
        columns = slice(strip * width, (strip + 1) * width)
        gram = lax.dot_general(
            grad[step], grad[strip], (((0,), (0,)), ((), ())), preferred_element_type=jnp.float32
        )
        new_right[0, :, columns] = DECAY * right[0, :, columns] + (1.0 - DECAY) * gram


def statistics(grad, left, right):
    strips, size, width = grad.shape
    rows = pl.BlockSpec((1, width, size), lambda t: (0, t, 0))
    return pl.pallas_call(
        statistics_kernel,
        grid=(strips,),
        out_shape=[jax.ShapeDtypeStruct(left.shape, left.dtype)] * 2,
        in_specs=[pl.BlockSpec((strips, size, width), lambda t: (0, 0, 0)), rows, rows],
        out_specs=[rows, rows],
        compiler_params=params(32),
        cost_estimate=pl.CostEstimate(flops=4 * size**3, bytes_accessed=18 * size * size, transcendentals=0),
        name="statistics",
    )(grad, left, right)


def pick_kernel(owners, returned, out, gathered, sem, *, columns, size, steps):
    groups = out.shape[0] // steps
    copies = []
    for step in range(steps):
        band = pl.ds(step * groups, groups)
        for group in range(step * groups, (step + 1) * groups):
            for column in range(columns):
                piece = returned[owners[group * columns + column]]
                gathered[group, :, column * size : (column + 1) * size] = piece
        copies.append(pltpu.make_async_copy(gathered.at[band], out.at[band], sem.at[step]))
        copies[-1].start()
    for copy in copies:
        copy.wait()


def pick(owners, returned, groups, columns, steps=6):
    _, rows, size = returned.shape
    shape = (groups, rows, columns * size)
    return pl.pallas_call(
        functools.partial(pick_kernel, columns=columns, size=size, steps=steps),
        out_shape=pltpu.HBM(shape, returned.dtype),
        in_specs=[pl.BlockSpec(memory_space=pltpu.SMEM), pl.BlockSpec(memory_space=pltpu.VMEM)],
        out_specs=pl.BlockSpec(memory_space=pltpu.HBM),
        scratch_shapes=[pltpu.VMEM(shape, returned.dtype), pltpu.SemaphoreType.DMA((steps,))],
        compiler_params=params(16),
        name="pick",
    )(owners, returned)


def body(grads, stat_left, stat_right, root_left, root_right, owner_block):
    reps = lax.axis_size("rep")
    devices = lax.axis_size("fsdp") * reps
    size = stat_left.shape[1]
    groups, full_width = grads.shape[1], grads.shape[3]
    columns = full_width // size
    width = size // reps
    across = [(r, r ^ 1) for r in range(reps)]
    mirror = [(r, reps - 1 - r) for r in range(reps)]
    orders = ((across, mirror), (mirror, across))

    matches = owner_block[None, :] == lax.iota(jnp.int32, groups * columns)[:, None]
    owners = jnp.sum(jnp.where(matches, lax.iota(jnp.int32, devices)[None, :], 0), axis=1)

    stages = len(STAGE_GROUPS)
    spans, start = [], 0
    for count in STAGE_GROUPS:
        for _ in range(2):
            spans.append((start, count))
            start += count
    parts = range(2 * stages)
    pairs = [(2 * stage, 2 * stage + 1) for stage in range(stages)]
    sizes = (columns, reps, width)
    packed = [part for pair in pairs for part in pack(grads, pair, spans, False, *sizes)]
    own = pack(grads, tuple(parts), spans, True, *sizes)
    packed[-2:], own = lax.optimization_barrier((packed[-2:], own))
    firsts = [lax.ppermute(packed[part], "rep", orders[part % 2][0]) for part in parts]
    seconds = [
        lax.ppermute(first_sum(own[part], firsts[part]), "rep", orders[part % 2][1]) for part in parts
    ]
    terms = list(zip(own, firsts, seconds))
    pieces = None
    for pair in pairs:
        pieces = second_sum(owners, terms, pair, spans, devices, pieces)
    grad_block = lax.all_to_all(pieces, ("rep", "fsdp"), split_axis=0, concat_axis=0, tiled=True)
    grad_block = grad_block.reshape(reps, size, width)
    update_block = block_update(root_left, grad_block, root_right)
    returned = lax.all_to_all(
        update_block.reshape(devices, size // devices, size),
        ("rep", "fsdp"),
        split_axis=0,
        concat_axis=0,
        tiled=True,
    )
    new_left, new_right = statistics(grad_block, stat_left, stat_right)
    return (new_left, new_right, pick(owners, returned, groups, columns))


def solution(mesh):
    in_specs = (
        P("rep", None, "fsdp", None),
        P(("rep", "fsdp"), None, None),
        P(("rep", "fsdp"), None, None),
        P(("rep", "fsdp"), None, None),
        P(("rep", "fsdp"), None, None),
        P(),
    )
    out_specs = (
        P(("rep", "fsdp"), None, None),
        P(("rep", "fsdp"), None, None),
        P(None, ("rep", "fsdp"), None),
    )
    return jax.shard_map(body, mesh=mesh, in_specs=in_specs, out_specs=out_specs, check_vma=False)
```

```python
import functools

import jax
import jax.numpy as jnp
from jax import lax
from jax.experimental import pallas as pl
from jax.experimental.pallas import tpu as pltpu
from jax.sharding import PartitionSpec as P

DECAY = 0.95
EPSILON = 1e-06
MIB = 1 << 20
STAGE_GROUPS = (2, 2, 2)


def params(mib):
    return pltpu.CompilerParams(vmem_limit_bytes=mib * MIB)


def first_partner(part, me, reps):
    return (me ^ 1, reps - 1 - me)[part % 2]


def second_partner(part, me, reps):
    return (reps - 1 - me, me ^ 1)[part % 2]


def pack_kernel(grads, *rest, parts, spans, own, columns, reps, width):
    outs, sem = rest[:-1], rest[-1]
    me = lax.axis_index("rep")
    copies = []
    for out, part in zip(outs, parts):
        start, groups = spans[part]
        target = me if own else first_partner(part, me, reps)
        for which, strip in enumerate((target, second_partner(part, target, reps))):
            for column in range(columns):
                offset = pl.multiple_of((column * reps + strip) * width, width)
                copies.append(
                    pltpu.make_async_copy(
                        grads.at[0, pl.ds(start, groups), :, pl.ds(offset, width)],
                        out.at[which, column],
                        sem.at[len(copies)],
                    )
                )
    for copy in copies:
        copy.start()
    for copy in copies:
        copy.wait()


def pack(grads, parts, spans, own, columns, reps, width):
    return pl.pallas_call(
        functools.partial(
            pack_kernel, parts=parts, spans=spans, own=own, columns=columns, reps=reps, width=width
        ),
        out_shape=[
            jax.ShapeDtypeStruct((2, columns, spans[part][1], grads.shape[2], width), grads.dtype) for part in parts
        ],
        in_specs=[pl.BlockSpec(memory_space=pltpu.HBM)],
        out_specs=[pl.BlockSpec(memory_space=pl.ANY)] * len(parts),
        scratch_shapes=[pltpu.SemaphoreType.DMA((2 * columns * len(parts),))],
        compiler_params=params(16),
        name="pack_own" if own else "pack",
    )(pltpu.with_memory_space_constraint(grads, pltpu.HBM))


def first_sum_kernel(own, received, sending):
    _, columns, groups, _, _ = own.shape
    for column in range(columns):
        for group in range(groups):
            total = own[1, column, group].astype(jnp.float32) + received[1, column, group].astype(jnp.float32)
            sending[column, group] = total.astype(sending.dtype)


def first_sum(own, received):
    return pl.pallas_call(
        first_sum_kernel,
        out_shape=jax.ShapeDtypeStruct(own.shape[1:], own.dtype),
        in_specs=[pl.BlockSpec(memory_space=pltpu.VMEM)] * 2,
        out_specs=pl.BlockSpec(memory_space=pltpu.VMEM),
        compiler_params=params(16),
        name="first_sum",
    )(own, received)


def second_sum_kernel(owners, *refs, parts, spans, columns, initial):
    out = refs[-1]
    if initial:
        out[...] = jnp.zeros_like(out)
    for index, part in enumerate(parts):
        own, first, second = refs[3 * index : 3 * index + 3]
        start, groups = spans[part]
        for group in range(groups):
            for column in range(columns):
                owner = owners[(start + group) * columns + column]
                total = own[0, column, group].astype(jnp.float32) + first[0, column, group].astype(jnp.float32)
                total += second[column, group].astype(jnp.float32)
                out[owner] = total.astype(out.dtype)


def second_sum(owners, terms, parts, spans, devices, before=None):
    _, columns, _, height, width = terms[0][0].shape
    arrays = [array for part in parts for array in terms[part]]
    aliases = {}
    if before is not None:
        arrays.append(before)
        aliases = {len(arrays): 0}
    return pl.pallas_call(
        functools.partial(
            second_sum_kernel, parts=parts, spans=spans, columns=columns, initial=before is None
        ),
        out_shape=jax.ShapeDtypeStruct((devices, height, width), arrays[0].dtype),
        in_specs=[pl.BlockSpec(memory_space=pltpu.SMEM)] + [pl.BlockSpec(memory_space=pltpu.VMEM)] * len(arrays),
        out_specs=pl.BlockSpec(memory_space=pltpu.VMEM),
        input_output_aliases=aliases,
        compiler_params=params(16),
        name="second_sum",
    )(owners, *arrays)


def update_kernel(left, grad, right, out, precond, scaled, sem, *, tiles, out_tiles):
    strips, size, width = grad.shape
    rows = size // tiles
    grad_square = jnp.zeros((8, width), jnp.float32)
    square = jnp.zeros((8, size), jnp.float32)
    for tile in range(tiles):
        band = slice(tile * rows, (tile + 1) * rows)
        middle = jnp.concatenate(
            [
                jnp.dot(left[0, band, :], grad[strip], preferred_element_type=jnp.float32).astype(jnp.bfloat16)
                for strip in range(strips)
            ],
            axis=1,
        )
        for strip in range(tile * strips // tiles, (tile + 1) * strips // tiles):
            as_float = grad[strip].astype(jnp.float32)
            grad_square += jnp.sum((as_float * as_float).reshape(size // 8, 8, width), axis=0)
        part = jnp.dot(middle, right[0], preferred_element_type=jnp.float32)
        precond[band, :] = part
        square += jnp.sum((part * part).reshape(rows // 8, 8, size), axis=0)
    entries = size * size
    mean_grad = jnp.full((8, 128), jnp.sum(grad_square) / entries)
    mean_precond = jnp.full((8, 128), jnp.sum(square) / entries)
    scale = jnp.sqrt(mean_grad / (mean_precond + EPSILON))[0:1, 0:1]
    eighth = size // (2 * out_tiles)
    edges = [0] + list(range(eighth, size, 2 * eighth)) + [size]
    copies = []
    for tile, (start, end) in enumerate(zip(edges[:-1], edges[1:])):
        band = slice(start, end)
        scaled[band, :] = (precond[band, :] * scale).astype(out.dtype)
        copies.append(pltpu.make_async_copy(scaled.at[band, :], out.at[band, :], sem.at[tile]))
        copies[-1].start()
    for copy in copies:
        copy.wait()


def block_update(left, grad, right, tiles=2, out_tiles=4):
    strips, size, width = grad.shape
    return pl.pallas_call(
        functools.partial(update_kernel, tiles=tiles, out_tiles=out_tiles),
        out_shape=pltpu.HBM((size, size), jnp.bfloat16),
        in_specs=[pl.BlockSpec(memory_space=pltpu.VMEM)] * 3,
        out_specs=pl.BlockSpec(memory_space=pltpu.HBM),
        scratch_shapes=[
            pltpu.VMEM((size, size), jnp.float32),
            pltpu.VMEM((size, size), jnp.bfloat16),
            pltpu.SemaphoreType.DMA((out_tiles + 1,)),
        ],
        compiler_params=params(32),
        cost_estimate=pl.CostEstimate(flops=4 * size**3, bytes_accessed=8 * size * size, transcendentals=0),
        name="block_update",
    )(left, grad, right)


def statistics_kernel(grad, left, right, new_left, new_right):
    step = pl.program_id(0)
    strips, size, width = grad.shape
    rows = pl.ds(pl.multiple_of(step * width, width), width)
    gram = jnp.zeros((width, size), jnp.float32)
    for strip in range(strips):
        gram += lax.dot_general(
            grad[strip, rows, :], grad[strip], (((1,), (1,)), ((), ())), preferred_element_type=jnp.float32
        )
    new_left[0] = DECAY * left[0] + (1.0 - DECAY) * gram
    for strip in range(strips):
        columns = slice(strip * width, (strip + 1) * width)
        gram = lax.dot_general(
            grad[step], grad[strip], (((0,), (0,)), ((), ())), preferred_element_type=jnp.float32
        )
        new_right[0, :, columns] = DECAY * right[0, :, columns] + (1.0 - DECAY) * gram


def statistics(grad, left, right):
    strips, size, width = grad.shape
    rows = pl.BlockSpec((1, width, size), lambda t: (0, t, 0))
    return pl.pallas_call(
        statistics_kernel,
        grid=(strips,),
        out_shape=[jax.ShapeDtypeStruct(left.shape, left.dtype)] * 2,
        in_specs=[pl.BlockSpec((strips, size, width), lambda t: (0, 0, 0)), rows, rows],
        out_specs=[rows, rows],
        compiler_params=params(32),
        cost_estimate=pl.CostEstimate(flops=4 * size**3, bytes_accessed=18 * size * size, transcendentals=0),
        name="statistics",
    )(grad, left, right)


def pick_kernel(owners, returned, out, gathered, sem, *, columns, size, steps):
    groups = out.shape[0] // steps
    copies = []
    for step in range(steps):
        band = pl.ds(step * groups, groups)
        for group in range(step * groups, (step + 1) * groups):
            for column in range(columns):
                piece = returned[owners[group * columns + column]]
                gathered[group, :, column * size : (column + 1) * size] = piece
        copies.append(pltpu.make_async_copy(gathered.at[band], out.at[band], sem.at[step]))
        copies[-1].start()
    for copy in copies:
        copy.wait()


def pick(owners, returned, groups, columns, steps=6):
    _, rows, size = returned.shape
    shape = (groups, rows, columns * size)
    return pl.pallas_call(
        functools.partial(pick_kernel, columns=columns, size=size, steps=steps),
        out_shape=pltpu.HBM(shape, returned.dtype),
        in_specs=[pl.BlockSpec(memory_space=pltpu.SMEM), pl.BlockSpec(memory_space=pltpu.VMEM)],
        out_specs=pl.BlockSpec(memory_space=pltpu.HBM),
        scratch_shapes=[pltpu.VMEM(shape, returned.dtype), pltpu.SemaphoreType.DMA((steps,))],
        compiler_params=params(16),
        name="pick",
    )(owners, returned)


def body(grads, stat_left, stat_right, root_left, root_right, owner_block):
    reps = lax.axis_size("rep")
    devices = lax.axis_size("fsdp") * reps
    size = stat_left.shape[1]
    groups, full_width = grads.shape[1], grads.shape[3]
    columns = full_width // size
    width = size // reps
    across = [(r, r ^ 1) for r in range(reps)]
    mirror = [(r, reps - 1 - r) for r in range(reps)]
    orders = ((across, mirror), (mirror, across))

    matches = owner_block[None, :] == lax.iota(jnp.int32, groups * columns)[:, None]
    owners = jnp.sum(jnp.where(matches, lax.iota(jnp.int32, devices)[None, :], 0), axis=1)

    stages = len(STAGE_GROUPS)
    spans, start = [], 0
    for count in STAGE_GROUPS:
        for _ in range(2):
            spans.append((start, count))
            start += count
    parts = range(2 * stages)
    pairs = [(2 * stage, 2 * stage + 1) for stage in range(stages)]
    sizes = (columns, reps, width)
    packed = [part for pair in pairs for part in pack(grads, pair, spans, False, *sizes)]
    firsts = [lax.ppermute(packed[part], "rep", orders[part % 2][0]) for part in parts]
    own = pack(grads, tuple(parts), spans, True, *sizes)
    seconds = [
        lax.ppermute(first_sum(own[part], firsts[part]), "rep", orders[part % 2][1]) for part in parts
    ]
    terms = list(zip(own, firsts, seconds))
    pieces = None
    for pair in pairs:
        pieces = second_sum(owners, terms, pair, spans, devices, pieces)
    grad_block = lax.all_to_all(pieces, ("rep", "fsdp"), split_axis=0, concat_axis=0, tiled=True)
    grad_block = grad_block.reshape(reps, size, width)
    update_block = block_update(root_left, grad_block, root_right)
    returned = lax.all_to_all(
        update_block.reshape(devices, size // devices, size),
        ("rep", "fsdp"),
        split_axis=0,
        concat_axis=0,
        tiled=True,
    )
    new_left, new_right = statistics(grad_block, stat_left, stat_right)
    return (new_left, new_right, pick(owners, returned, groups, columns))


def solution(mesh):
    in_specs = (
        P("rep", None, "fsdp", None),
        P(("rep", "fsdp"), None, None),
        P(("rep", "fsdp"), None, None),
        P(("rep", "fsdp"), None, None),
        P(("rep", "fsdp"), None, None),
        P(),
    )
    out_specs = (
        P(("rep", "fsdp"), None, None),
        P(("rep", "fsdp"), None, None),
        P(None, ("rep", "fsdp"), None),
    )
    return jax.shard_map(body, mesh=mesh, in_specs=in_specs, out_specs=out_specs, check_vma=False)
```
